32 devices in a mesh: lon: 16 (over z, y, x), lat: 2 (over core).
Axes of the slice: x: 2, y: 2, z: 4, core: 2. Of those that a mesh axis runs over, the one named last changes fastest.
Arguments:
- field: bfloat16 [128, 256, 256], P('lat', 'lon'), may hold values from -6 to 6
- cotangent: bfloat16 [128, 256, 256], P('lat', 'lon'), may hold values from -6 to 6
- lon_kernel: float32 [31, 256], replicated, may hold values from -1 to 1
- lat_kernel: float32 [31, 256], replicated, may hold values from -1 to 1
- w_in: bfloat16 [256, 1024], replicated, may hold values from -0.375 to 0.375
- w_out: bfloat16 [1024, 256], replicated, may hold values from -0.1875 to 0.1875
Outputs:
- result: bfloat16 [128, 256, 256], P('lat', 'lon')
- d_field: bfloat16 [128, 256, 256], P('lat', 'lon')
- grad_in: float32 [256, 1024], replicated
- grad_out: float32 [1024, 256], replicated
- grad_lat: float32 [31, 256], replicated
- grad_lon: float32 [31, 256], replicated
The draws below stay inside these ranges and needn't reach their ends.
All inputs are finite; a program needn't handle non-finite values.
Results may differ from the reference program's by a relative error of at most 0.007.
Values may be sent and summed in bfloat16 or wider, within the bound.
A program may use at most 64 MiB of HBM per device.

```python
import math
import jax
import jax.numpy as jnp
from jax import lax

C = 256
H = 1024
KW = 31
HALF = 15
LAT_DEV = 64
NLON = 256
NLAT = 128
N_LAT = 2


def steps_of(key, dims, split, smallest, largest):
    level, own = 1.0, jax.random.fold_in(key, 6)
    for dim, blocks in split:
        draws = jnp.exp(jax.random.uniform(jax.random.fold_in(own, dim), (blocks,), jnp.float32, smallest / len(split), largest / len(split)))
        level = level * jnp.repeat(draws, dims[dim] // blocks).reshape([-1 if axis == dim else 1 for axis in range(len(dims))])
    return level


def gaussian(stream_key, dims, scale, bound, pieces=(), kind=jnp.bfloat16):
    factor_of = steps_of(stream_key, dims, pieces, -0.22, 0.18) if pieces else 1.0
    values = jax.random.normal(stream_key, dims, jnp.float32) * scale * factor_of
    return jnp.minimum(jnp.maximum(values, -bound), bound).astype(kind)


def setup_inputs(seed: int = 0) -> dict:
    arg_keys = jax.random.split(jax.random.key(seed), 7)
    return {
        "field": gaussian(arg_keys[0], (NLAT, NLON, C), 1.0, 6.0, ((0, 2), (1, 16))),
        "cotangent": gaussian(arg_keys[1], (NLAT, NLON, C), 1.0, 6.0, ((0, 2), (1, 16))),
        "lon_kernel": gaussian(arg_keys[2], (KW, C), KW ** -0.5, 1.0, (), jnp.float32),
        "lat_kernel": gaussian(arg_keys[3], (KW, C), KW ** -0.5, 1.0, (), jnp.float32),
        "w_in": gaussian(arg_keys[4], (C, H), C ** -0.5, 0.375),
        "w_out": gaussian(arg_keys[5], (H, C), H ** -0.5, 0.1875),
    }


def kernel_taps(padded, kernel, along, length):
    total = None
    for offset in range(kernel.shape[0]):
        piece = lax.slice_in_dim(padded, offset, offset + length, axis=along).astype(jnp.float32) * kernel[offset]
        total = piece if total is None else total + piece
    return total

def kernel_grad(padded, grad, along, length):
    grad_wide = grad.astype(jnp.float32)
    rows_out = []
    for offset in range(KW):
        piece = lax.slice_in_dim(padded, offset, offset + length, axis=along).astype(jnp.float32)
        rows_out.append(lax.optimization_barrier(jnp.sum(piece * grad_wide, axis=(0, 1))))
    return jnp.stack(rows_out)

def mlp_block(mixed_rows, field_rows, cot_rows, w_in, w_out, scale):
    rms = jnp.sqrt(lax.optimization_barrier(jnp.mean(mixed_rows * mixed_rows, axis=-1, keepdims=True)) + 1e-06)
    unit = mixed_rows / rms
    normed = unit.astype(jnp.bfloat16)
    pre = jnp.dot(normed, w_in, preferred_element_type=jnp.float32)
    act_wide, gelu_back = jax.vjp(jax.nn.gelu, pre)
    act = act_wide.astype(jnp.bfloat16)
    result = (field_rows.astype(jnp.float32) + jnp.dot(act, w_out, preferred_element_type=jnp.float32)).astype(jnp.bfloat16)
    d_act = lax.dot_general(cot_rows, w_out, (((1,), (1,)), ((), ())), preferred_element_type=jnp.float32)
    d_pre = gelu_back(d_act)[0].astype(jnp.bfloat16)
    grad_out = scale * lax.dot_general(act, cot_rows, (((0,), (0,)), ((), ())), preferred_element_type=jnp.float32)
    grad_in = scale * lax.dot_general(normed, d_pre, (((0,), (0,)), ((), ())), preferred_element_type=jnp.float32)
    d_norm = lax.dot_general(d_pre, w_in, (((1,), (1,)), ((), ())), preferred_element_type=jnp.float32)
    d_mixed = ((d_norm - unit * lax.optimization_barrier(jnp.mean(d_norm * unit, axis=-1, keepdims=True))) / rms).astype(jnp.bfloat16)
    return (result, d_mixed, grad_in, grad_out)

def cycle_pad(values):
    return jnp.concatenate([values[:, -HALF:], values, values[:, :HALF]], axis=1)

def band_pad(values):
    return jnp.pad(values, ((HALF, HALF), (0, 0), (0, 0)))

def reference(field, cotangent, lon_kernel, lat_kernel, w_in, w_out):
    scale = 1.0 / math.sqrt(NLAT * NLON)
    field_cycle = cycle_pad(field)
    along = kernel_taps(field_cycle, lon_kernel, 1, NLON).astype(jnp.bfloat16)
    along_band = band_pad(along)
    mixed = kernel_taps(along_band, lat_kernel, 0, NLAT)
    blocks = N_LAT
    rows_blk = LAT_DEV * NLON

    def block_step(carry, inputs):
        mixed_blk, field_blk, cot_blk = inputs
        result_blk, dmix_blk, gin, gout = mlp_block(mixed_blk, field_blk, cot_blk, w_in, w_out, scale)
        return ((carry[0] + gin, carry[1] + gout), (result_blk, dmix_blk))
    start = (jnp.zeros((C, H), jnp.float32), jnp.zeros((H, C), jnp.float32))
    (grad_in, grad_out), (result, d_mixed) = lax.scan(block_step, start, (mixed.reshape(blocks, rows_blk, C), field.reshape(blocks, rows_blk, C), cotangent.reshape(blocks, rows_blk, C)))
    result = result.reshape(NLAT, NLON, C)
    d_mixed = d_mixed.reshape(NLAT, NLON, C)
    grad_lat = scale * kernel_grad(along_band, d_mixed, 0, NLAT)
    d_along = kernel_taps(band_pad(d_mixed), lat_kernel[::-1], 0, NLAT).astype(jnp.bfloat16)
    grad_lon = scale * kernel_grad(field_cycle, d_along, 1, NLON)
    d_field = (cotangent.astype(jnp.float32) + kernel_taps(cycle_pad(d_along), lon_kernel[::-1], 1, NLON)).astype(jnp.bfloat16)
    return (result, d_field, grad_in, grad_out, grad_lat, grad_lon)
```

```python
import functools
import math

import jax
import jax.numpy as jnp
from jax import lax
from jax.experimental import pallas as pl
from jax.experimental.pallas import tpu as pltpu
from jax.sharding import PartitionSpec as P

KW = 31
HALF = 15
BF = jnp.bfloat16
F32 = jnp.float32
CH = 4
ROOT = math.sqrt(2.0 / math.pi)


def kernel(
    n_lon, n_lat, subs,
    field, cot, lon_k, lat_k, w_in, w_out,
    result, d_field, out_big, out_small,
    xpad, ypad, aband, dband, mixed, abf, dalbf, frecv, drecv, arecv, mrecv,
    wlon, wlat, w_in_t, w_out_t, act, dpre, normed, dmbf,
    part_b, lrecv_b, pair_b, nrecv_b, all_b,
    part_s, lrecv_s, pair_s, nrecv_s, all_s,
    f_ss, f_rs, d_ss, d_rs, a_ss, a_rs, m_ss, m_rs,
    b_lss, b_lrs, b_nss, b_nrs, b_ass, b_ars, b_gss, b_grs,
    s_lss, s_lrs, s_nss, s_nrs, s_ass, s_ars, s_gss, s_grs,
):
    lat_dev, lon_dev, chans = field.shape
    halves = chans // 128
    hidden = w_in.shape[1]
    rows = lat_dev // CH
    me = lax.axis_index("lon")
    my = lax.axis_index("lat")
    right = lax.rem(me + 1, n_lon)
    left = lax.rem(me + n_lon - 1, n_lon)

    def remote(src, dst, ss, rs, lon, lat):
        return pltpu.make_async_remote_copy(
            src_ref=src, dst_ref=dst, send_sem=ss, recv_sem=rs,
            device_id=(lon, lat), device_id_type=pl.DeviceIdType.MESH,
        )

    barrier = pltpu.get_barrier_semaphore()

    @pl.loop(1, n_lon)
    def _(p):
        pl.semaphore_signal(barrier, inc=1, device_id=(lax.rem(me + p, n_lon), my),
                            device_id_type=pl.DeviceIdType.MESH)

    @pl.loop(1, n_lat)
    def _(p):
        pl.semaphore_signal(barrier, inc=1, device_id=(me, lax.rem(my + p, n_lat)),
                            device_id_type=pl.DeviceIdType.MESH)

    pl.semaphore_wait(barrier, n_lon + n_lat - 2)

    def lon_halo(src, dst, ss, rs, q):
        part = pl.ds(q * rows, rows)
        return (
            remote(src.at[part], dst.at[0, part], ss.at[0, q], rs.at[0, q], right, my),
            remote(src.at[part], dst.at[1, part], ss.at[1, q], rs.at[1, q], left, my),
        )

    def widen(src, pad, row0, count, col):
        @pl.loop(0, count)
        def _(i):
            v = src[row0 + i].astype(F32)
            for h in range(halves):
                pad[h, row0 + i, col:col + lon_dev, :] = v[:, h * 128:(h + 1) * 128]

    field_halo = [lon_halo(field, frecv, f_ss, f_rs, q) for q in range(CH)]
    for pair in field_halo:
        for c in pair:
            c.start()

    for h in range(halves):
        for k in range(KW):
            lanes = slice(h * 128, (h + 1) * 128)
            wlon[h, k] = jnp.broadcast_to(lon_k[k:k + 1, lanes], (8, 128))
            wlat[h, k] = jnp.broadcast_to(lat_k[k:k + 1, lanes], (8, 128))
    for b in range(hidden // 256):
        blk = slice(b * 256, (b + 1) * 256)
        w_in_t[blk, :] = w_in[:, blk].T
        w_out_t[:, blk] = w_out[blk, :].T
    widen(field, xpad, 0, lat_dev, lon_dev)

    def lon_taps(pad, wide, i, h, flip):
        lo = jnp.zeros((8, 128), F32)
        hi = jnp.zeros((8, 128), F32)
        for k in range(KW):
            off = 31 - k if flip else k + 1
            lo = lo + pad[h, i, off:off + 8, :] * wide[k]
            hi = hi + pad[h, i, off + 8:off + 16, :] * wide[k]
        return jnp.concatenate([lo, hi], axis=0)

    band = [[0, HALF], [HALF + lat_dev, HALF]]
    for q in range(CH):
        for side in range(2):
            field_halo[q][side].wait_recv()
            widen(frecv.at[side], xpad, q * rows, rows, 2 * lon_dev * side)
        for h in range(halves):
            wide = [wlon[h, k] for k in range(KW)]

            @pl.loop(q * rows, (q + 1) * rows)
            def _(i):
                v = lon_taps(xpad, wide, i, h, False).astype(BF)
                abf[i, :, h * 128:(h + 1) * 128] = v
                aband[h, HALF + i] = v.astype(F32)

    def lat_start(src, dst, ss, rs):
        @pl.when(my + 1 < n_lat)
        def _():
            remote(src.at[pl.ds(lat_dev - HALF, HALF)], dst.at[0], ss.at[0], rs.at[0], me, my + 1).start()

        @pl.when(my > 0)
        def _():
            remote(src.at[pl.ds(0, HALF)], dst.at[1], ss.at[1], rs.at[1], me, my - 1).start()

    def lat_finish(src, dst, wide, ss, rs):
        for side, has in ((0, my > 0), (1, my + 1 < n_lat)):
            base = side * (HALF + lat_dev)

            @pl.when(has)
            def _():
                remote(src.at[pl.ds(0, HALF)], dst.at[side], ss.at[side], rs.at[side], me, lax.rem(my + 1, n_lat)).wait_recv()

                @pl.loop(0, HALF)
                def _(i):
                    v = dst[side, i].astype(F32)
                    for h in range(halves):
                        wide[h, base + i] = v[:, h * 128:(h + 1) * 128]

            @pl.when(jnp.logical_not(has))
            def _():
                @pl.loop(0, HALF)
                def _(i):
                    for h in range(halves):
                        wide[h, base + i] = jnp.zeros((lon_dev, 128), F32)

    def lat_sent(src, dst, ss, rs):
        @pl.when(my + 1 < n_lat)
        def _():
            remote(src.at[pl.ds(lat_dev - HALF, HALF)], dst.at[0], ss.at[0], rs.at[0], me, my + 1).wait_send()

        @pl.when(my > 0)
        def _():
            remote(src.at[pl.ds(0, HALF)], dst.at[1], ss.at[1], rs.at[1], me, my - 1).wait_send()

    GROUP = 4

    def lat_taps(wide_ref, ws, h, row0, flip):
        acc = [jnp.zeros((lon_dev, 128), F32)] * GROUP
        for j in range(KW - 1 + GROUP):
            x = wide_ref[h, row0 + j]
            for r in range(GROUP):
                k = j - r
                if 0 <= k < KW:
                    acc[r] = acc[r] + x * ws[KW - 1 - k if flip else k]
        return acc

    def lat_weights(h):
        return [jnp.concatenate([wlat[h, k]] * 2, axis=0) for k in range(KW)]

    lat_start(abf, arecv, a_ss, a_rs)
    lat_finish(abf, arecv, aband, a_ss, a_rs)
    for h in range(halves):
        ws = lat_weights(h)

        @pl.loop(0, lat_dev // GROUP)
        def _(g):
            acc = lat_taps(aband, ws, h, g * GROUP, False)
            for r in range(GROUP):
                mixed[g * GROUP + r, :, h * 128:(h + 1) * 128] = acc[r]

    tile = 16
    cells = tile * lon_dev

    @pl.loop(0, lat_dev // tile)
    def _(t):
        lats = pl.ds(t * tile, tile)
        rws = pl.ds(pl.multiple_of(t * cells, cells), cells)
        mix = mixed[lats].reshape(cells, chans)
        inv = 1.0 / jnp.sqrt(jnp.mean(mix * mix, axis=-1, keepdims=True) + 1e-6)
        unit = mix * inv
        nrm = unit.astype(BF)
        normed[rws, :] = nrm
        ct = cot[lats].reshape(cells, chans)
        res = field[lats].reshape(cells, chans).astype(F32)
        dn = jnp.zeros((cells, chans), F32)
        for b in range(hidden // 256):
            blk = slice(b * 256, (b + 1) * 256)
            x = jnp.dot(nrm, w_in[:, blk], preferred_element_type=F32)
            da = jnp.dot(ct, w_out_t[:, blk], preferred_element_type=F32)
            xx = x * x
            th = jnp.tanh(x * (ROOT + (ROOT * 0.044715) * xx))
            hp = 0.5 + 0.5 * th
            a = (x * hp).astype(BF)
            slope = hp + (0.5 * x) * (1.0 - th * th) * (ROOT + (3.0 * ROOT * 0.044715) * xx)
            dp = (da * slope).astype(BF)
            act[rws, blk] = a
            dpre[rws, blk] = dp
            res = res + jnp.dot(a, w_out[blk, :], preferred_element_type=F32)
            dn = dn + jnp.dot(dp, w_in_t[blk, :], preferred_element_type=F32)
        result[lats] = res.astype(BF).reshape(tile, lon_dev, chans)
        dm = ((dn - unit * jnp.mean(dn * unit, axis=-1, keepdims=True)) * inv).astype(BF)
        dm = dm.reshape(tile, lon_dev, chans)
        abf_m = dm.astype(F32)
        for h in range(halves):
            dband[h, pl.ds(HALF + t * tile, tile)] = abf_m[:, :, h * 128:(h + 1) * 128]
        dmbf[lats] = dm

    lat_start(dmbf, mrecv, m_ss, m_rs)

    for b in range(hidden // 256):
        blk = slice(b * 256, (b + 1) * 256)
        part_b[blk, :] = lax.dot_general(
            act[:, blk], cot[...].reshape(lat_dev * lon_dev, chans),
            (((0,), (0,)), ((), ())), preferred_element_type=F32).astype(BF)
        part_b[hidden + b * 256:hidden + (b + 1) * 256, :] = lax.dot_general(
            normed[...], dpre[:, blk],
            (((0,), (0,)), ((), ())), preferred_element_type=F32).astype(BF)

    def reduction(part, lrecv, pair, nrecv, whole, sub, lss, lrs, nss, nrs, ass, ars, gss, grs):
        per_lat = part.shape[0] // n_lat
        owners = per_lat // sub
        mine = pl.multiple_of(my * per_lat, 16)
        has = me < owners

        def lat_copy(p):
            to = lax.rem(my + p, n_lat)
            src = part.at[pl.ds(pl.multiple_of(to * per_lat, 16), per_lat)]
            return remote(src, lrecv.at[p - 1], lss.at[p - 1], lrs.at[p - 1], me, to)

        def lon_copy(p):
            to = lax.rem(me + p, n_lon)
            src = pair.at[pl.ds(pl.multiple_of(lax.rem(to, owners) * sub, 16), sub)]
            return to, remote(src, nrecv.at[p - 1], nss.at[p - 1], nrs.at[p - 1], to, my)

        def own_rows(lon):
            return pl.ds(pl.multiple_of(mine + lax.rem(lon, owners) * sub, 16), sub)

        def gather_copy(p, lon):
            ref = whole.at[own_rows(lon)]
            return remote(ref, ref, ass.at[p - 1], ars.at[p - 1], lax.rem(me + p, n_lon), my)

        def spread_copy(p, lat):
            ref = whole.at[pl.ds(pl.multiple_of(lat * per_lat, 16), per_lat)]
            return remote(ref, ref, gss.at[p - 1], grs.at[p - 1], me, lax.rem(my + p, n_lat))

        def step1():
            @pl.loop(1, n_lat)
            def _(p):
                lat_copy(p).start()

        def step2():
            @pl.loop(1, n_lat)
            def _(p):
                lat_copy(p).wait_recv()
            total = part[pl.ds(mine, per_lat), :].astype(F32)
            for p in range(1, n_lat):
                total = total + lrecv[p - 1].astype(F32)
            pair[...] = total.astype(BF)

            @pl.loop(1, n_lon)
            def _(p):
                to, c = lon_copy(p)

                @pl.when(to < owners)
                def _():
                    c.start()

        def step3():
            @pl.when(has)
            def _():
                @pl.loop(1, n_lon)
                def _(p):
                    lon_copy(p)[1].wait_recv()
                rows_own = pl.ds(pl.multiple_of(lax.rem(me, owners) * sub, 16), sub)
                total = pair[rows_own, :].astype(F32)
                total = lax.fori_loop(
                    0, n_lon - 1, lambda p, v: v + nrecv[p].astype(F32), total)
                whole[own_rows(me), :] = total.astype(BF)

                @pl.loop(1, n_lon)
                def _(p):
                    gather_copy(p, me).start()

        def step4():
            @pl.loop(1, n_lon)
            def _(p):
                source = lax.rem(me + n_lon - p, n_lon)

                @pl.when(source < owners)
                def _():
                    gather_copy(p, source).wait_recv()

            @pl.loop(1, n_lat)
            def _(p):
                spread_copy(p, my).start()

        def step5():
            @pl.loop(1, n_lat)
            def _(p):
                spread_copy(p, lax.rem(my + n_lat - p, n_lat)).wait_recv()

        def done():
            @pl.loop(1, n_lat)
            def _(p):
                lat_copy(p).wait_send()
                spread_copy(p, my).wait_send()

            @pl.loop(1, n_lon)
            def _(p):
                to, c = lon_copy(p)

                @pl.when(to < owners)
                def _():
                    c.wait_send()

                @pl.when(has)
                def _():
                    gather_copy(p, me).wait_send()

        return step1, step2, step3, step4, step5, done

    big = reduction(part_b, lrecv_b, pair_b, nrecv_b, all_b, subs[0],
                    b_lss, b_lrs, b_nss, b_nrs, b_ass, b_ars, b_gss, b_grs)
    small = reduction(part_s, lrecv_s, pair_s, nrecv_s, all_s, subs[1],
                      s_lss, s_lrs, s_nss, s_nrs, s_ass, s_ars, s_gss, s_grs)
    big[0]()

    lat_finish(dmbf, mrecv, dband, m_ss, m_rs)
    d_halo = [lon_halo(dalbf, drecv, d_ss, d_rs, q) for q in range(CH)]
    for q in range(CH):
        for h in range(halves):
            ws = lat_weights(h)

            @pl.loop(0, rows // GROUP)
            def _(g):
                row0 = q * rows + g * GROUP
                acc = lat_taps(dband, ws, h, row0, True)
                for r in range(GROUP):
                    v = acc[r].astype(BF)
                    dalbf[row0 + r, :, h * 128:(h + 1) * 128] = v
                    ypad[h, row0 + r, lon_dev:2 * lon_dev, :] = v.astype(F32)
        for c in d_halo[q]:
            c.start()
    big[1]()

    part_s[...] = jnp.zeros(part_s.shape, BF)

    def tap_grads(load_d, load_x, base):
        for h in range(halves):
            def body(i, accs):
                d = load_d(h, i)
                d0, d1 = d[:8], d[8:]
                out = []
                for k in range(KW):
                    x0, x1 = load_x(h, i, k)
                    out.append(accs[k] + (x0 * d0 + x1 * d1))
                return tuple(out)

            accs = lax.fori_loop(0, lat_dev, body, (jnp.zeros((8, 128), F32),) * KW)
            sums = [jnp.sum(a, axis=0, keepdims=True) for a in accs]
            sums.append(jnp.zeros((1, 128), F32))
            part_s[base:base + 32, h * 128:(h + 1) * 128] = jnp.concatenate(sums, axis=0).astype(BF)

    def lat_x(h, i, k):
        v = aband[h, i + k]
        return v[:8], v[8:]

    tap_grads(lambda h, i: dband[h, HALF + i], lat_x, 0)
    tap_grads(
        lambda h, i: ypad[h, i, lon_dev:2 * lon_dev, :],
        lambda h, i, k: (xpad[h, i, k + 1:k + 9, :], xpad[h, i, k + 9:k + 17, :]),
        32,
    )
    small[0]()
    big[2]()
    small[1]()

    for q in range(CH):
        for side in range(2):
            d_halo[q][side].wait_recv()
            widen(drecv.at[side], ypad, q * rows, rows, 2 * lon_dev * side)
        if q == 1:
            small[2]()
        if q == 2:
            big[3]()
        for h in range(halves):
            wide = [wlon[h, k] for k in range(KW)]
            lanes = slice(h * 128, (h + 1) * 128)

            @pl.loop(q * rows, (q + 1) * rows)
            def _(i):
                v = lon_taps(ypad, wide, i, h, True)
                d_field[i, :, lanes] = (cot[i, :, lanes].astype(F32) + v).astype(BF)

    small[3]()
    big[4]()
    out_big[...] = all_b[...]
    small[4]()
    out_small[...] = all_s[...]
    big[5]()
    small[5]()
    for pair in field_halo + d_halo:
        for c in pair:
            c.wait_send()
    lat_sent(abf, arecv, a_ss, a_rs)
    lat_sent(dmbf, mrecv, m_ss, m_rs)


def split_rows(total, n_lon, n_lat):
    per_lat = total // n_lat
    sub = max(16, per_lat // n_lon)
    assert per_lat % sub == 0 and sub % 16 == 0 and per_lat // sub <= n_lon
    return per_lat, sub


def on_device(n_lon, n_lat, field, cotangent, lon_kernel, lat_kernel, w_in, w_out):
    lat_dev, lon_dev, chans = field.shape
    hidden = w_in.shape[1]
    halves = chans // 128
    cells = lat_dev * lon_dev
    scale = 1.0 / math.sqrt(cells * n_lon * n_lat)
    big = 2 * hidden
    small = max(64, 16 * n_lat)
    big_lat, big_sub = split_rows(big, n_lon, n_lat)
    small_lat, small_sub = split_rows(small, n_lon, n_lat)
    sem = pltpu.SemaphoreType.DMA

    def buffers(total, per_lat, sub):
        return [
            pltpu.VMEM((total, chans), BF),
            pltpu.VMEM((max(n_lat - 1, 1), per_lat, chans), BF),
            pltpu.VMEM((per_lat, chans), BF),
            pltpu.VMEM((n_lon - 1, sub, chans), BF),
            pltpu.VMEM((total, chans), BF),
        ]

    sems = [sem((n_lat,))] * 2 + [sem((n_lon,))] * 4 + [sem((n_lat,))] * 2
    block = (lat_dev, lon_dev, chans)
    result, d_field, all_big, all_small = pl.pallas_call(
        functools.partial(kernel, n_lon, n_lat, (big_sub, small_sub)),
        out_shape=[
            jax.ShapeDtypeStruct(block, BF),
            jax.ShapeDtypeStruct(block, BF),
            jax.ShapeDtypeStruct((big, chans), BF),
            jax.ShapeDtypeStruct((small, chans), BF),
        ],
        in_specs=[pl.BlockSpec(memory_space=pltpu.VMEM)] * 6,
        out_specs=[pl.BlockSpec(memory_space=pltpu.VMEM)] * 4,
        scratch_shapes=[
            pltpu.VMEM((halves, lat_dev, 3 * lon_dev, 128), F32),
            pltpu.VMEM((halves, lat_dev, 3 * lon_dev, 128), F32),
            pltpu.VMEM((halves, lat_dev + 2 * HALF, lon_dev, 128), F32),
            pltpu.VMEM((halves, lat_dev + 2 * HALF, lon_dev, 128), F32),
            pltpu.VMEM(block, F32),
            pltpu.VMEM(block, BF),
            pltpu.VMEM(block, BF),
            pltpu.VMEM((2,) + block, BF),
            pltpu.VMEM((2,) + block, BF),
            pltpu.VMEM((2, HALF, lon_dev, chans), BF),
            pltpu.VMEM((2, HALF, lon_dev, chans), BF),
            pltpu.VMEM((halves, KW, 8, 128), F32),
            pltpu.VMEM((halves, KW, 8, 128), F32),
            pltpu.VMEM((hidden, chans), BF),
            pltpu.VMEM((chans, hidden), BF),
            pltpu.VMEM((cells, hidden), BF),
            pltpu.VMEM((cells, hidden), BF),
            pltpu.VMEM((cells, chans), BF),
            pltpu.VMEM(block, BF),
        ]
        + buffers(big, big_lat, big_sub)
        + buffers(small, small_lat, small_sub)
        + [sem((2, CH))] * 4
        + [sem((2,))] * 4
        + sems
        + sems,
        compiler_params=pltpu.CompilerParams(
            collective_id=0, has_side_effects=True, vmem_limit_bytes=56 * 1024 * 1024
        ),
    )(field, cotangent, lon_kernel, lat_kernel, w_in, w_out)
    grad_out = scale * all_big[:hidden].astype(F32)
    grad_in = scale * (
        all_big[hidden:].reshape(hidden // 256, chans, 256).transpose(1, 0, 2)
        .reshape(chans, hidden).astype(F32)
    )
    grad_lat = scale * all_small[:KW].astype(F32)
    grad_lon = scale * all_small[32:32 + KW].astype(F32)
    return (result, d_field, grad_in, grad_out, grad_lat, grad_lon)


def solution(mesh):
    placed = (P("lat", "lon", None), P("lat", "lon", None), P(), P(), P(), P())
    return jax.shard_map(
        functools.partial(on_device, mesh.shape["lon"], mesh.shape["lat"]),
        mesh=mesh,
        in_specs=placed,
        out_specs=(P("lat", "lon", None), P("lat", "lon", None), P(), P(), P(), P()),
        check_vma=False,
    )
```

```python
import functools
import math

import jax
import jax.numpy as jnp
from jax import lax
from jax.experimental import pallas as pl
from jax.experimental.pallas import tpu as pltpu
from jax.sharding import PartitionSpec as P

KW = 31
HALF = 15
BF = jnp.bfloat16
F32 = jnp.float32
CH = 4
ROOT = math.sqrt(2.0 / math.pi)


def kernel(
    n_lon, n_lat, subs,
    field, cot, lon_k, lat_k, w_in, w_out,
    result, d_field, out_big, out_small,
    xpad, ypad, aband, dband, mixed, abf, dalbf, frecv, drecv, arecv, mrecv,
    wlon, wlat, w_in_t, w_out_t, act, dpre, normed, dmbf,
    part_b, lrecv_b, pair_b, nrecv_b, all_b,
    part_s, lrecv_s, pair_s, nrecv_s, all_s,
    f_ss, f_rs, d_ss, d_rs, a_ss, a_rs, m_ss, m_rs,
    b_lss, b_lrs, b_nss, b_nrs, b_ass, b_ars, b_gss, b_grs,
    s_lss, s_lrs, s_nss, s_nrs, s_ass, s_ars, s_gss, s_grs,
):
    lat_dev, lon_dev, chans = field.shape
    halves = chans // 128
    hidden = w_in.shape[1]
    rows = lat_dev // CH
    me = lax.axis_index("lon")
    my = lax.axis_index("lat")
    right = lax.rem(me + 1, n_lon)
    left = lax.rem(me + n_lon - 1, n_lon)

    def remote(src, dst, ss, rs, lon, lat):
        return pltpu.make_async_remote_copy(
            src_ref=src, dst_ref=dst, send_sem=ss, recv_sem=rs,
            device_id=(lon, lat), device_id_type=pl.DeviceIdType.MESH,
        )

    barrier = pltpu.get_barrier_semaphore()

    @pl.loop(1, n_lon)
    def _(p):
        pl.semaphore_signal(barrier, inc=1, device_id=(lax.rem(me + p, n_lon), my),
                            device_id_type=pl.DeviceIdType.MESH)

    @pl.loop(1, n_lat)
    def _(p):
        pl.semaphore_signal(barrier, inc=1, device_id=(me, lax.rem(my + p, n_lat)),
                            device_id_type=pl.DeviceIdType.MESH)

    pl.semaphore_wait(barrier, n_lon + n_lat - 2)

    def lon_halo(src, dst, ss, rs, q):
        part = pl.ds(q * rows, rows)
        return (
            remote(src.at[part], dst.at[0, part], ss.at[0, q], rs.at[0, q], right, my),
            remote(src.at[part], dst.at[1, part], ss.at[1, q], rs.at[1, q], left, my),
        )

    def widen(src, pad, row0, count, col):
        @pl.loop(0, count)
        def _(i):
            v = src[row0 + i].astype(F32)
            for h in range(halves):
                pad[h, row0 + i, col:col + lon_dev, :] = v[:, h * 128:(h + 1) * 128]

    even = lax.rem(my, 2) == 0

    def order(q):
        return jnp.where(even, CH - 1 - q, q)

    for q in range(CH):
        for c in lon_halo(field, frecv, f_ss, f_rs, order(q)):
            c.start()

    for h in range(halves):
        for k in range(KW):
            lanes = slice(h * 128, (h + 1) * 128)
            wlon[h, k] = jnp.broadcast_to(lon_k[k:k + 1, lanes], (8, 128))
            wlat[h, k] = jnp.broadcast_to(lat_k[k:k + 1, lanes], (8, 128))
    for b in range(hidden // 256):
        blk = slice(b * 256, (b + 1) * 256)
        w_in_t[blk, :] = w_in[:, blk].T
        w_out_t[:, blk] = w_out[blk, :].T
    widen(field, xpad, 0, lat_dev, lon_dev)

    def lon_taps(pad, wide, i, h, flip):
        lo = jnp.zeros((8, 128), F32)
        hi = jnp.zeros((8, 128), F32)
        for k in range(KW):
            off = 31 - k if flip else k + 1
            lo = lo + pad[h, i, off:off + 8, :] * wide[k]
            hi = hi + pad[h, i, off + 8:off + 16, :] * wide[k]
        return jnp.concatenate([lo, hi], axis=0)

    def edge_start(q, src, dst, ss, rs):
        @pl.when(jnp.logical_and(q == CH - 1, my + 1 < n_lat))
        def _():
            remote(src.at[pl.ds(lat_dev - HALF, HALF)], dst.at[0], ss.at[0], rs.at[0], me, my + 1).start()

        @pl.when(jnp.logical_and(q == 0, my > 0))
        def _():
            remote(src.at[pl.ds(0, HALF)], dst.at[1], ss.at[1], rs.at[1], me, my - 1).start()

    def edge_finish(q, src, dst, wide, ss, rs):
        for side, has in ((0, my > 0), (1, my + 1 < n_lat)):
            base = side * (HALF + lat_dev)
            here = q == side * (CH - 1)

            @pl.when(jnp.logical_and(here, has))
            def _():
                remote(src.at[pl.ds(0, HALF)], dst.at[side], ss.at[side], rs.at[side], me, lax.rem(my + 1, n_lat)).wait_recv()

                @pl.loop(0, HALF)
                def _(i):
                    v = dst[side, i].astype(F32)
                    for h in range(halves):
                        wide[h, base + i] = v[:, h * 128:(h + 1) * 128]

            @pl.when(jnp.logical_and(here, jnp.logical_not(has)))
            def _():
                @pl.loop(0, HALF)
                def _(i):
                    for h in range(halves):
                        wide[h, base + i] = jnp.zeros((lon_dev, 128), F32)

    def lon_forward(q):
        for c in lon_halo(field, frecv, f_ss, f_rs, q):
            c.wait_recv()
        for side in range(2):
            widen(frecv.at[side], xpad, q * rows, rows, 2 * lon_dev * side)
        for h in range(halves):
            wide = [wlon[h, k] for k in range(KW)]

            @pl.loop(0, rows)
            def _(r):
                i = q * rows + r
                v = lon_taps(xpad, wide, i, h, False).astype(BF)
                abf[i, :, h * 128:(h + 1) * 128] = v
                aband[h, HALF + i] = v.astype(F32)
        edge_start(q, abf, arecv, a_ss, a_rs)

    def lat_sent(src, dst, ss, rs):
        @pl.when(my + 1 < n_lat)
        def _():
            remote(src.at[pl.ds(lat_dev - HALF, HALF)], dst.at[0], ss.at[0], rs.at[0], me, my + 1).wait_send()

        @pl.when(my > 0)
        def _():
            remote(src.at[pl.ds(0, HALF)], dst.at[1], ss.at[1], rs.at[1], me, my - 1).wait_send()

    GROUP = 4

    def lat_taps(wide_ref, ws, h, row0, flip):
        acc = [jnp.zeros((lon_dev, 128), F32)] * GROUP
        for j in range(KW - 1 + GROUP):
            x = wide_ref[h, row0 + j]
            for r in range(GROUP):
                k = j - r
                if 0 <= k < KW:
                    acc[r] = acc[r] + x * ws[KW - 1 - k if flip else k]
        return acc

    def lat_weights(h):
        return [jnp.concatenate([wlat[h, k]] * 2, axis=0) for k in range(KW)]

    tile = rows
    cells = tile * lon_dev

    def mlp(t):
        edge_finish(t, abf, arecv, aband, a_ss, a_rs)
        for h in range(halves):
            ws = lat_weights(h)

            @pl.loop(0, tile // GROUP)
            def _(g):
                row0 = t * tile + g * GROUP
                acc = lat_taps(aband, ws, h, row0, False)
                for r in range(GROUP):
                    mixed[row0 + r, :, h * 128:(h + 1) * 128] = acc[r]

        lats = pl.ds(t * tile, tile)
        rws = pl.ds(pl.multiple_of(t * cells, cells), cells)
        mix = mixed[lats].reshape(cells, chans)
        inv = 1.0 / jnp.sqrt(jnp.mean(mix * mix, axis=-1, keepdims=True) + 1e-6)
        unit = mix * inv
        nrm = unit.astype(BF)
        normed[rws, :] = nrm
        ct = cot[lats].reshape(cells, chans)
        res = field[lats].reshape(cells, chans).astype(F32)
        dn = jnp.zeros((cells, chans), F32)
        for b in range(hidden // 256):
            blk = slice(b * 256, (b + 1) * 256)
            x = jnp.dot(nrm, w_in[:, blk], preferred_element_type=F32)
            da = jnp.dot(ct, w_out_t[:, blk], preferred_element_type=F32)
            xx = x * x
            th = jnp.tanh(x * (ROOT + (ROOT * 0.044715) * xx))
            hp = 0.5 + 0.5 * th
            a = (x * hp).astype(BF)
            slope = hp + (0.5 * x) * (1.0 - th * th) * (ROOT + (3.0 * ROOT * 0.044715) * xx)
            dp = (da * slope).astype(BF)
            act[rws, blk] = a
            dpre[rws, blk] = dp
            res = res + jnp.dot(a, w_out[blk, :], preferred_element_type=F32)
            dn = dn + jnp.dot(dp, w_in_t[blk, :], preferred_element_type=F32)
        result[lats] = res.astype(BF).reshape(tile, lon_dev, chans)
        dm = ((dn - unit * jnp.mean(dn * unit, axis=-1, keepdims=True)) * inv).astype(BF)
        dm = dm.reshape(tile, lon_dev, chans)
        abf_m = dm.astype(F32)
        for h in range(halves):
            dband[h, pl.ds(HALF + t * tile, tile)] = abf_m[:, :, h * 128:(h + 1) * 128]
        dmbf[lats] = dm
        edge_start(t, dmbf, mrecv, m_ss, m_rs)

    def lat_backward(q):
        edge_finish(q, dmbf, mrecv, dband, m_ss, m_rs)
        for h in range(halves):
            ws = lat_weights(h)

            @pl.loop(0, rows // GROUP)
            def _(g):
                row0 = q * rows + g * GROUP
                acc = lat_taps(dband, ws, h, row0, True)
                for r in range(GROUP):
                    v = acc[r].astype(BF)
                    dalbf[row0 + r, :, h * 128:(h + 1) * 128] = v
                    ypad[h, row0 + r, lon_dev:2 * lon_dev, :] = v.astype(F32)
        for c in lon_halo(dalbf, drecv, d_ss, d_rs, q):
            c.start()

    @pl.loop(0, CH + 1)
    def _(s):
        @pl.when(s < CH)
        def _():
            lon_forward(order(s))

        @pl.when(s >= 1)
        def _():
            mlp(order(s - 1))

        @pl.when(s >= 2)
        def _():
            lat_backward(order(s - 2))

    for b in range(hidden // 256):
        blk = slice(b * 256, (b + 1) * 256)
        part_b[blk, :] = lax.dot_general(
            act[:, blk], cot[...].reshape(lat_dev * lon_dev, chans),
            (((0,), (0,)), ((), ())), preferred_element_type=F32).astype(BF)
        part_b[hidden + b * 256:hidden + (b + 1) * 256, :] = lax.dot_general(
            normed[...], dpre[:, blk],
            (((0,), (0,)), ((), ())), preferred_element_type=F32).astype(BF)

    def reduction(part, lrecv, pair, nrecv, whole, sub, lss, lrs, nss, nrs, ass, ars, gss, grs):
        per_lat = part.shape[0] // n_lat
        owners = per_lat // sub
        mine = pl.multiple_of(my * per_lat, 16)
        has = me < owners

        def lat_copy(p):
            to = lax.rem(my + p, n_lat)
            src = part.at[pl.ds(pl.multiple_of(to * per_lat, 16), per_lat)]
            return remote(src, lrecv.at[p - 1], lss.at[p - 1], lrs.at[p - 1], me, to)

        def lon_copy(p):
            to = lax.rem(me + p, n_lon)
            src = pair.at[pl.ds(pl.multiple_of(lax.rem(to, owners) * sub, 16), sub)]
            return to, remote(src, nrecv.at[p - 1], nss.at[p - 1], nrs.at[p - 1], to, my)

        def own_rows(lon):
            return pl.ds(pl.multiple_of(mine + lax.rem(lon, owners) * sub, 16), sub)

        def gather_copy(p, lon):
            ref = whole.at[own_rows(lon)]
            return remote(ref, ref, ass.at[p - 1], ars.at[p - 1], lax.rem(me + p, n_lon), my)

        def spread_copy(p, lat):
            ref = whole.at[pl.ds(pl.multiple_of(lat * per_lat, 16), per_lat)]
            return remote(ref, ref, gss.at[p - 1], grs.at[p - 1], me, lax.rem(my + p, n_lat))

        def step1():
            @pl.loop(1, n_lat)
            def _(p):
                lat_copy(p).start()

        def step2():
            @pl.loop(1, n_lat)
            def _(p):
                lat_copy(p).wait_recv()
            total = part[pl.ds(mine, per_lat), :].astype(F32)
            for p in range(1, n_lat):
                total = total + lrecv[p - 1].astype(F32)
            pair[...] = total.astype(BF)

            @pl.loop(1, n_lon)
            def _(p):
                to, c = lon_copy(p)

                @pl.when(to < owners)
                def _():
                    c.start()

        def step3():
            @pl.when(has)
            def _():
                @pl.loop(1, n_lon)
                def _(p):
                    lon_copy(p)[1].wait_recv()
                rows_own = pl.ds(pl.multiple_of(lax.rem(me, owners) * sub, 16), sub)
                total = pair[rows_own, :].astype(F32)
                total = lax.fori_loop(
                    0, n_lon - 1, lambda p, v: v + nrecv[p].astype(F32), total)
                whole[own_rows(me), :] = total.astype(BF)

                @pl.loop(1, n_lon)
                def _(p):
                    gather_copy(p, me).start()

        def step4():
            @pl.loop(1, n_lon)
            def _(p):
                source = lax.rem(me + n_lon - p, n_lon)

                @pl.when(source < owners)
                def _():
                    gather_copy(p, source).wait_recv()

            @pl.loop(1, n_lat)
            def _(p):
                spread_copy(p, my).start()

        def step5():
            @pl.loop(1, n_lat)
            def _(p):
                spread_copy(p, lax.rem(my + n_lat - p, n_lat)).wait_recv()

        def done():
            @pl.loop(1, n_lat)
            def _(p):
                lat_copy(p).wait_send()
                spread_copy(p, my).wait_send()

            @pl.loop(1, n_lon)
            def _(p):
                to, c = lon_copy(p)

                @pl.when(to < owners)
                def _():
                    c.wait_send()

                @pl.when(has)
                def _():
                    gather_copy(p, me).wait_send()

        return step1, step2, step3, step4, step5, done

    big = reduction(part_b, lrecv_b, pair_b, nrecv_b, all_b, subs[0],
                    b_lss, b_lrs, b_nss, b_nrs, b_ass, b_ars, b_gss, b_grs)
    small = reduction(part_s, lrecv_s, pair_s, nrecv_s, all_s, subs[1],
                      s_lss, s_lrs, s_nss, s_nrs, s_ass, s_ars, s_gss, s_grs)
    big[0]()

    big[1]()
    lat_backward(order(CH - 1))

    part_s[...] = jnp.zeros(part_s.shape, BF)

    def tap_grads(load_d, load_x, base):
        for h in range(halves):
            def body(i, accs):
                d = load_d(h, i)
                d0, d1 = d[:8], d[8:]
                out = []
                for k in range(KW):
                    x0, x1 = load_x(h, i, k)
                    out.append(accs[k] + (x0 * d0 + x1 * d1))
                return tuple(out)

            accs = lax.fori_loop(0, lat_dev, body, (jnp.zeros((8, 128), F32),) * KW)
            sums = [jnp.sum(a, axis=0, keepdims=True) for a in accs]
            sums.append(jnp.zeros((1, 128), F32))
            part_s[base:base + 32, h * 128:(h + 1) * 128] = jnp.concatenate(sums, axis=0).astype(BF)

    def lat_x(h, i, k):
        v = aband[h, i + k]
        return v[:8], v[8:]

    tap_grads(lambda h, i: dband[h, HALF + i], lat_x, 0)
    tap_grads(
        lambda h, i: ypad[h, i, lon_dev:2 * lon_dev, :],
        lambda h, i, k: (xpad[h, i, k + 1:k + 9, :], xpad[h, i, k + 9:k + 17, :]),
        32,
    )
    small[0]()

    def lon_backward(q):
        for c in lon_halo(dalbf, drecv, d_ss, d_rs, q):
            c.wait_recv()
        for side in range(2):
            widen(drecv.at[side], ypad, q * rows, rows, 2 * lon_dev * side)
        for h in range(halves):
            wide = [wlon[h, k] for k in range(KW)]
            lanes = slice(h * 128, (h + 1) * 128)

            @pl.loop(0, rows)
            def _(r):
                i = q * rows + r
                v = lon_taps(ypad, wide, i, h, True)
                d_field[i, :, lanes] = (cot[i, :, lanes].astype(F32) + v).astype(BF)

    big[2]()
    small[1]()
    lon_backward(order(0))
    lon_backward(order(1))
    small[2]()
    lon_backward(order(2))
    big[3]()
    small[3]()
    lon_backward(order(3))
    small[4]()
    out_small[...] = all_s[...]
    big[4]()
    out_big[...] = all_b[...]
    big[5]()
    small[5]()
    for q in range(CH):
        for c in lon_halo(field, frecv, f_ss, f_rs, q) + lon_halo(dalbf, drecv, d_ss, d_rs, q):
            c.wait_send()
    lat_sent(abf, arecv, a_ss, a_rs)
    lat_sent(dmbf, mrecv, m_ss, m_rs)


def split_rows(total, n_lon, n_lat):
    per_lat = total // n_lat
    sub = max(16, per_lat // n_lon)
    assert per_lat % sub == 0 and sub % 16 == 0 and per_lat // sub <= n_lon
    return per_lat, sub


def on_device(n_lon, n_lat, field, cotangent, lon_kernel, lat_kernel, w_in, w_out):
    lat_dev, lon_dev, chans = field.shape
    hidden = w_in.shape[1]
    halves = chans // 128
    cells = lat_dev * lon_dev
    scale = 1.0 / math.sqrt(cells * n_lon * n_lat)
    big = 2 * hidden
    small = max(64, 16 * n_lat)
    big_lat, big_sub = split_rows(big, n_lon, n_lat)
    small_lat, small_sub = split_rows(small, n_lon, n_lat)
    sem = pltpu.SemaphoreType.DMA

    def buffers(total, per_lat, sub):
        return [
            pltpu.VMEM((total, chans), BF),
            pltpu.VMEM((max(n_lat - 1, 1), per_lat, chans), BF),
            pltpu.VMEM((per_lat, chans), BF),
            pltpu.VMEM((n_lon - 1, sub, chans), BF),
            pltpu.VMEM((total, chans), BF),
        ]

    sems = [sem((n_lat,))] * 2 + [sem((n_lon,))] * 4 + [sem((n_lat,))] * 2
    block = (lat_dev, lon_dev, chans)
    result, d_field, all_big, all_small = pl.pallas_call(
        functools.partial(kernel, n_lon, n_lat, (big_sub, small_sub)),
        out_shape=[
            jax.ShapeDtypeStruct(block, BF),
            jax.ShapeDtypeStruct(block, BF),
            jax.ShapeDtypeStruct((big, chans), BF),
            jax.ShapeDtypeStruct((small, chans), BF),
        ],
        in_specs=[pl.BlockSpec(memory_space=pltpu.VMEM)] * 6,
        out_specs=[pl.BlockSpec(memory_space=pltpu.VMEM)] * 4,
        scratch_shapes=[
            pltpu.VMEM((halves, lat_dev, 3 * lon_dev, 128), F32),
            pltpu.VMEM((halves, lat_dev, 3 * lon_dev, 128), F32),
            pltpu.VMEM((halves, lat_dev + 2 * HALF, lon_dev, 128), F32),
            pltpu.VMEM((halves, lat_dev + 2 * HALF, lon_dev, 128), F32),
            pltpu.VMEM(block, F32),
            pltpu.VMEM(block, BF),
            pltpu.VMEM(block, BF),
            pltpu.VMEM((2,) + block, BF),
            pltpu.VMEM((2,) + block, BF),
            pltpu.VMEM((2, HALF, lon_dev, chans), BF),
            pltpu.VMEM((2, HALF, lon_dev, chans), BF),
            pltpu.VMEM((halves, KW, 8, 128), F32),
            pltpu.VMEM((halves, KW, 8, 128), F32),
            pltpu.VMEM((hidden, chans), BF),
            pltpu.VMEM((chans, hidden), BF),
            pltpu.VMEM((cells, hidden), BF),
            pltpu.VMEM((cells, hidden), BF),
            pltpu.VMEM((cells, chans), BF),
            pltpu.VMEM(block, BF),
        ]
        + buffers(big, big_lat, big_sub)
        + buffers(small, small_lat, small_sub)
        + [sem((2, CH))] * 4
        + [sem((2,))] * 4
        + sems
        + sems,
        compiler_params=pltpu.CompilerParams(
            collective_id=0, has_side_effects=True, vmem_limit_bytes=56 * 1024 * 1024
        ),
    )(field, cotangent, lon_kernel, lat_kernel, w_in, w_out)
    grad_out = scale * all_big[:hidden].astype(F32)
    grad_in = scale * (
        all_big[hidden:].reshape(hidden // 256, chans, 256).transpose(1, 0, 2)
        .reshape(chans, hidden).astype(F32)
    )
    grad_lat = scale * all_small[:KW].astype(F32)
    grad_lon = scale * all_small[32:32 + KW].astype(F32)
    return (result, d_field, grad_in, grad_out, grad_lat, grad_lon)


def solution(mesh):
    placed = (P("lat", "lon", None), P("lat", "lon", None), P(), P(), P(), P())
    return jax.shard_map(
        functools.partial(on_device, mesh.shape["lon"], mesh.shape["lat"]),
        mesh=mesh,
        in_specs=placed,
        out_specs=(P("lat", "lon", None), P("lat", "lon", None), P(), P(), P(), P()),
        check_vma=False,
    )
```
